128 devices in a mesh: outer: 8 (over y, z_lo), inner: 16 (over x, z_hi, core).
Axes of the slice: x: 4, y: 4, z: 4 (z_hi: 2, z_lo: 2; z = z_hi * 2 + z_lo), core: 2. Of those that a mesh axis runs over, the one named last changes fastest.
Arguments:
- queries: bfloat16 [24576, 2048], P(('outer', 'inner')), may hold values from -160 to 160
- keys: bfloat16 [24576, 256], P(('outer', 'inner')), may hold values from -6 to 6
- values: bfloat16 [24576, 256], P(('outer', 'inner')), may hold values from -6 to 6
- span_order: int32 [256], replicated, may hold values from 0 to 255, as said below
- doc_lengths: int32 [4], replicated, may hold values from 1 to 12288, 24576 in all
Outputs:
- attended: bfloat16 [24576, 2048], P(('outer', 'inner'))
- log_sum: float32 [16, 24576], P(None, ('outer', 'inner'))
The draws below stay inside these ranges and needn't reach their ends.
Inputs may be any that keep to these rules, and one draw needn't show every extreme that they name: `span_order`: each device's two span slots (rows 2 d * 96 to (2 d + 2) * 96 - 1 for device d) hold spans c and 255 - c for some c, and every span appears exactly once.
All inputs are finite; a program needn't handle non-finite values.
Results may differ from the reference program's by a relative error of at most 0.0055.
Values may be sent and summed in bfloat16 or wider, within the bound.
No kernel may reach another device: no remote copies, remote signals or barrier semaphores. Data moves between devices by JAX's collectives and lax.ppermute only.
A program may use at most 128 MiB of HBM per device.

```python
import math
import jax
import jax.numpy as jnp
import numpy as np
from jax import lax

GROUPS = 2
QPG = 8
DH = 128
HEADS = 16
SPAN = 96
DOCS = 4
NSPAN = 256
TOKENS = 24576


def shared_keys(key):
    normal_part = jnp.clip(jax.random.normal(jax.random.fold_in(key, 11), (TOKENS, GROUPS * DH), jnp.float32), -6.0, 6.0)
    return normal_part


def draw_keys(key, part):
    result = shared_keys(key)
    return result.astype(jnp.bfloat16)


def draw_queries(key, part):
    key = jax.random.fold_in(key, 2)
    result = jnp.clip(2.5 * jax.random.normal(key, (TOKENS, HEADS * DH), jnp.float32), -12.0, 12.0)
    return result.astype(jnp.bfloat16)


def draw_span_order(key, part):
    key = jax.random.fold_in(key, 3)
    pairs = jax.random.permutation(key, NSPAN // 2).astype(jnp.int32)
    flips = jax.random.randint(jax.random.fold_in(key, 4), (NSPAN // 2,), 0, 2)
    first = jnp.where(flips == 1, pairs, NSPAN - 1 - pairs)
    second = NSPAN - 1 - first
    return jnp.stack([first, second], axis=1).reshape(NSPAN).astype(jnp.int32)


def block_scale(stream_key, shape, pieces, least, high):
    gain, own = 1.0, jax.random.fold_in(stream_key, 6)
    for dim, blocks in pieces:
        steps = jnp.exp(jax.random.uniform(jax.random.fold_in(own, dim), (blocks,), jnp.float32, least / len(pieces), high / len(pieces)))
        gain = gain * jnp.repeat(steps, shape[dim] // blocks).reshape([-1 if axis == dim else 1 for axis in range(len(shape))])
    return gain


def split_up(number_of, total, limit, skew):
    portions = [(1 << 20) // math.isqrt(standing ** skew) + 1 for standing in range(2, number_of + 1)]
    surplus, counts = total - limit - (number_of - 1), [1] * (number_of - 1)
    while surplus > 0:
        candidates = [i for i in range(number_of - 1) if counts[i] < limit]
        whole, left = sum([portions[i] for i in candidates]), surplus
        for i in candidates:
            extra = min(limit - counts[i], max(1, left * portions[i] // whole), surplus)
            counts[i] = counts[i] + extra
            surplus = surplus - extra
    return np.array([limit] + counts)


def uneven(key, count, total, reach, skew):
    if count == 2:
        one = jax.random.randint(key, (), max(1, total - reach), min(reach, total - 1) + 1)
        return jnp.stack([one, total - one])
    tallies = jnp.asarray(split_up(count, total, reach, skew), jnp.int32)
    twos = (count - 1) // 2
    giver, sink = tallies[1:1 + 2 * twos:2], tallies[2:2 + 2 * twos:2]
    slack = jnp.minimum(giver - 1, reach - sink)
    passed = jax.random.randint(jax.random.fold_in(key, 1), (twos,), 0, 1 << 20) % (slack + 1)
    tallies = tallies.at[1:1 + 2 * twos:2].set(giver - passed).at[2:2 + 2 * twos:2].set(sink + passed)
    return tallies[jax.random.permutation(jax.random.fold_in(key, 2), count)]


def centred(stream_key, extent, scale, limit, cuts=(), kind=jnp.bfloat16):
    level = block_scale(stream_key, extent, cuts, -0.22, 0.18) if cuts else 1.0
    entries = jax.random.normal(stream_key, extent, jnp.float32) * scale * level
    return jnp.minimum(jnp.maximum(entries, -limit), limit).astype(kind)


def setup_inputs(seed: int = 0) -> dict:
    arg_keys = jax.random.split(jax.random.key(seed), 6)
    queries = draw_queries(jax.random.fold_in(arg_keys[5], 71), 0)
    keys = draw_keys(jax.random.fold_in(arg_keys[5], 71), 0)
    values = centred(arg_keys[2], (TOKENS, GROUPS * DH), 1.0, 6.0, ((0, 128),))
    span_order = draw_span_order(jax.random.fold_in(arg_keys[5], 71), 0)
    doc_lengths = uneven(arg_keys[4], DOCS, TOKENS, TOKENS // 2, 2).astype(jnp.int32)
    return {"queries": queries, "keys": keys, "values": values, "span_order": span_order, "doc_lengths": doc_lengths}


rows_per_block = 128


def reference(queries, keys, values, span_order, doc_lengths):
    slot_ids = jnp.arange(TOKENS, dtype=jnp.int32)
    positions = span_order[slot_ids // SPAN] * SPAN + slot_ids % SPAN
    doc_ends = jnp.cumsum(doc_lengths)
    doc_start = jnp.sum(jnp.where(doc_ends[None, :] <= positions[:, None], doc_lengths[None, :], 0), axis=1)
    query_heads = queries.astype(jnp.float32).reshape(TOKENS, GROUPS, QPG, DH)
    key_heads = keys.astype(jnp.float32).reshape(TOKENS, GROUPS, DH)
    value_heads = values.astype(jnp.float32).reshape(TOKENS, GROUPS, DH)
    scale = 1.0 / (DH ** 0.5)

    def one_block(block_index):
        row_start = block_index * rows_per_block
        query_rows = lax.dynamic_slice_in_dim(query_heads, row_start, rows_per_block, 0)
        query_pos = lax.dynamic_slice_in_dim(positions, row_start, rows_per_block, 0)
        query_first = lax.dynamic_slice_in_dim(doc_start, row_start, rows_per_block, 0)
        scores = jnp.einsum("qgad,kgd->gaqk", query_rows, key_heads) * scale
        visible = (positions[None, :] <= query_pos[:, None]) & (positions[None, :] >= query_first[:, None])
        scores = jnp.where(visible[None, None], scores, -1e30)
        row_max = jnp.max(scores, axis=3)
        weights = jnp.where(visible[None, None], jnp.exp(scores - row_max[..., None]), 0.0)
        weight_sum = jnp.sum(weights, axis=3)
        rounded = lax.optimization_barrier(weights.astype(jnp.bfloat16)).astype(jnp.float32)
        summed = jnp.einsum("gaqk,kgd->gaqd", rounded, value_heads) / weight_sum[..., None]
        attended = summed.transpose(2, 0, 1, 3).reshape(rows_per_block, HEADS * DH).astype(jnp.bfloat16)
        log_sum = (row_max + jnp.log(weight_sum)).reshape(HEADS, rows_per_block)
        return attended, log_sum

    outputs, log_sums = lax.map(one_block, jnp.arange(TOKENS // rows_per_block, dtype=jnp.int32))
    return outputs.reshape(TOKENS, HEADS * DH), log_sums.transpose(1, 0, 2).reshape(HEADS, TOKENS)
```

```python
import functools
import itertools
import math

import jax
import jax.numpy as jnp
from jax import lax
from jax.experimental import pallas as pl
from jax.experimental.pallas import tpu as pltpu
from jax.sharding import PartitionSpec as P

DH = 128
SPAN = 96
QPG = 8
MROWS = QPG * SPAN
NSP = 2
GC = 4
NK = GC * SPAN
MT = 384
LOG2E = 1.0 / math.log(2.0)
SCALE2 = LOG2E / DH**0.5
M_INIT = -1e29
BIAS = -3e30
FAR = 1 << 24
AXES = ("outer", "inner")
STAGE_CHUNKS = (64, 128, 64)
NL = 136
F32, BF16 = jnp.float32, jnp.bfloat16


def device_id(x, y, z, c):
    return (y * 2 + z % 2) * 16 + x * 4 + (z // 2) * 2 + c


def permute(v, move):
    pairs = []
    for y, x, z, c in itertools.product(range(4), range(4), range(4), range(2)):
        pairs.append((device_id(x, y, z, c), device_id(*move(x, y, z, c))))
    return lax.ppermute(v, AXES, pairs)


def shift(v, axis, step0, step1):
    def move(x, y, z, c):
        step = step0 if c == 0 else step1
        if axis == "y":
            return x, (y + step) % 4, z, c
        return x, y, (z + step) % 4, c

    return permute(v, move)


def flip_x(v, bits):
    return permute(v, lambda x, y, z, c: (x ^ bits, y, z, c))


def swap_core(v):
    return permute(v, lambda x, y, z, c: (x, y, z, 1 - c))


def kernel(n_pieces, first, last, ids, kps, cnt, qb, docs, q_ref, *rest):
    pieces, rest = rest[:n_pieces], rest[n_pieces:]
    if not first:
        (m_in, l_in, a_in), rest = rest[:3], rest[3:]
    if last:
        (o_ref, lse_ref), rest = rest[:2], rest[2:]
    else:
        (m_out, l_out, a_out), rest = rest[:3], rest[3:]
    kv, qs, m_s, l_s, a_s, sems = rest
    sp = pl.program_id(0)

    def copies():
        at, out = 0, []
        for i, piece in enumerate(pieces):
            rows = piece.shape[0]
            out.append(pltpu.make_async_copy(piece, kv.at[pl.ds(at, rows)], sems.at[i]))
            at += rows
        return out

    @pl.when(sp == 0)
    def _():
        for copy in copies():
            copy.start()

    for h in range(QPG):
        qs[h * SPAN : (h + 1) * SPAN, :] = q_ref[:, h * DH : (h + 1) * DH]
    if first:
        m_s[...] = jnp.full_like(m_s, M_INIT)
        l_s[...] = jnp.zeros_like(l_s)
        a_s[...] = jnp.zeros_like(a_s)
    else:
        m_s[...] = m_in[0]
        l_s[...] = l_in[0]
        a_s[...] = a_in[0]

    @pl.when(sp == 0)
    def _():
        for copy in copies():
            copy.wait()

    def step(number, masked):
        base = number * GC
        starts = [pl.multiple_of(ids[sp, base + j] * SPAN, 32) for j in range(GC)]
        k = jnp.concatenate([kv[pl.ds(s, SPAN), 0:DH] for s in starts], axis=0)
        v = jnp.concatenate([kv[pl.ds(s, SPAN), DH : 2 * DH] for s in starts], axis=0)
        if masked:
            lane = lax.broadcasted_iota(jnp.int32, (SPAN, NK), 1)
            kpos = lane + kps[sp, base]
            for j in range(1, GC):
                kpos = jnp.where(lane >= j * SPAN, lane + (kps[sp, base + j] - j * SPAN), kpos)
            qpos = lax.broadcasted_iota(jnp.int32, (SPAN, NK), 0) + qb[sp]
            start = jnp.zeros((SPAN, NK), jnp.int32)
            for j in range(4):
                start = start + jnp.where(qpos >= docs[j], docs[4 + j], 0)
            bias = jnp.where((kpos <= qpos) & (kpos >= start), 0.0, BIAS)
        for t in range(MROWS // MT):
            rows = slice(t * MT, (t + 1) * MT)
            s = lax.dot_general(qs[rows, :], k, (((1,), (1,)), ((), ())), preferred_element_type=F32)
            if masked:
                s = (s.reshape(MT // SPAN, SPAN, NK) + bias[None]).reshape(MT, NK)
            m_old = m_s[rows, :]
            m_new = jnp.maximum(m_old, jnp.max(s, axis=1, keepdims=True) * SCALE2)
            factor = jnp.exp2(m_old - m_new)
            p = [jnp.exp2(s[:, j * DH : (j + 1) * DH] * SCALE2 - m_new) for j in range(NK // DH)]
            m_s[rows, :] = m_new
            l_s[rows, :] = l_s[rows, :] * factor + functools.reduce(jnp.add, p)
            w = jnp.concatenate([e.astype(BF16) for e in p], axis=1)
            a_s[rows, :] = a_s[rows, :] * factor + jnp.dot(w, v, preferred_element_type=F32)

    n_plain = cnt[sp, 0] // GC
    n_all = (cnt[sp, 1] + (GC - 1)) // GC

    @pl.loop(0, n_plain)
    def _(number):
        step(number, False)

    @pl.loop(n_plain, n_all)
    def _(number):
        step(number, True)

    if last:
        for h in range(QPG):
            rows = slice(h * SPAN, (h + 1) * SPAN)
            total = jnp.sum(l_s[rows, :], axis=1, keepdims=True)
            o_ref[:, h * DH : (h + 1) * DH] = (a_s[rows, :] / total).astype(BF16)
            lse = m_s[rows, :] * math.log(2.0) + jnp.log(total)
            lse_ref[0, h : h + 1, :] = jnp.transpose(lse)[0:1, :]
    else:
        m_out[0] = m_s[...]
        l_out[0] = l_s[...]
        a_out[0] = a_s[...]


def attend(lists, docs, q, pieces, state, first, last):
    ids, kps, cnt, qb = lists
    total = sum(p.shape[0] for p in pieces)
    state_spec = pl.BlockSpec((1, MROWS, DH), lambda i, *_: (i, 0, 0))
    state_shape = jax.ShapeDtypeStruct((NSP, MROWS, DH), F32)
    if last:
        out_specs = (
            pl.BlockSpec((SPAN, QPG * DH), lambda i, *_: (i, 0)),
            pl.BlockSpec((1, QPG, SPAN), lambda i, *_: (i, 0, 0)),
        )
        out_shape = (
            jax.ShapeDtypeStruct((NSP * SPAN, QPG * DH), BF16),
            jax.ShapeDtypeStruct((NSP, QPG, SPAN), F32),
        )
    else:
        out_specs, out_shape = (state_spec,) * 3, (state_shape,) * 3
    pairs = NSP * MROWS * total // 5
    return pl.pallas_call(
        functools.partial(kernel, len(pieces), first, last),
        grid_spec=pltpu.PrefetchScalarGridSpec(
            num_scalar_prefetch=5,
            grid=(NSP,),
            in_specs=[pl.BlockSpec((SPAN, QPG * DH), lambda i, *_: (i, 0))]
            + [pl.BlockSpec(memory_space=pl.ANY)] * len(pieces)
            + ([] if first else [state_spec] * 3),
            out_specs=out_specs,
            scratch_shapes=[
                pltpu.VMEM((total, 2 * DH), BF16),
                pltpu.VMEM((MROWS, DH), BF16),
                pltpu.VMEM((MROWS, DH), F32),
                pltpu.VMEM((MROWS, DH), F32),
                pltpu.VMEM((MROWS, DH), F32),
                pltpu.SemaphoreType.DMA((len(pieces),)),
            ],
        ),
        out_shape=out_shape,
        compiler_params=pltpu.CompilerParams(vmem_limit_bytes=40 * 1024 * 1024),
        cost_estimate=pl.CostEstimate(flops=8 * pairs * DH, bytes_accessed=total * 512, transcendentals=pairs),
    )(ids, kps, cnt, qb, docs, q, *pieces, *(() if first else state))


def rows_of(table, slots):
    hit = slots[..., None] == jnp.arange(table.shape[0], dtype=jnp.int32)
    return jnp.sum(jnp.where(hit, table, 0), axis=-1)


def make_lists(key_spans, query_spans, ends, lengths):
    n = key_spans.shape[0]
    stage = jnp.concatenate([jnp.full((c,), i, jnp.int32) for i, c in enumerate(STAGE_CHUNKS)])
    offset = jnp.concatenate(
        [jnp.full((c,), sum(STAGE_CHUNKS[:i]), jnp.int32) for i, c in enumerate(STAGE_CHUNKS)]
    )
    a = (key_spans * SPAN)[None, :]
    b = query_spans * SPAN

    def starts(pos):
        return jnp.sum(jnp.where(ends[None, :] <= pos[:, None], lengths[None, :], 0), axis=1)

    first, final = starts(b)[:, None], starts(b + SPAN - 1)[:, None]
    seen = (a <= b[:, None] + SPAN - 1) & (a + SPAN - 1 >= first)
    whole = (a + SPAN - 1 <= b[:, None]) & (a >= final)
    cut = seen & ~whole
    number = jnp.arange(n, dtype=jnp.int32)
    same = stage[:, None] == stage[None, :]
    before = same & (number[None, :] < number[:, None])
    n_whole = jnp.sum((whole[:, None, :] & same[None]).astype(jnp.int32), axis=2)
    place_whole = jnp.sum((whole[:, None, :] & before[None]).astype(jnp.int32), axis=2)
    place_cut = n_whole + jnp.sum((cut[:, None, :] & before[None]).astype(jnp.int32), axis=2)
    place = jnp.where(whole, place_whole, jnp.where(cut, place_cut, FAR))
    slot = jnp.arange(NL, dtype=jnp.int32)
    out = []
    for i, c in enumerate(STAGE_CHUNKS):
        lo = sum(STAGE_CHUNKS[:i])
        part = slice(lo, lo + c)
        hit = place[:, None, part] == slot[None, :, None]
        ids = jnp.sum(jnp.where(hit, number[None, None, :c], 0), axis=2)
        kps = jnp.sum(jnp.where(hit, a[:, None, part], 0), axis=2)
        kps = jnp.where(jnp.any(hit, axis=2), kps, FAR)
        n_full = jnp.sum(whole[:, part].astype(jnp.int32), axis=1)
        n_all = n_full + jnp.sum(cut[:, part].astype(jnp.int32), axis=1)
        out.append((ids, kps, jnp.stack([n_full, n_all], axis=1)))
    return out


def gather_ring(v, axis, core):
    below = shift(v, axis, 1, 1)
    above = shift(v, axis, -1, -1)
    return below, above, lambda: shift(jnp.where(core == 0, below, above), axis, 1, -1)


def on_device(queries, keys, values, span_order, doc_lengths):
    outer, inner = lax.axis_index("outer"), lax.axis_index("inner")
    x, core = inner // 4, inner % 2
    y, z = outer // 2, (inner // 2) % 2 * 2 + outer % 2
    odd = x % 2 == 1

    group0 = jnp.concatenate([keys[:, :DH], values[:, :DH]], axis=1)
    group1 = jnp.concatenate([keys[:, DH:], values[:, DH:]], axis=1)
    mine, other = jnp.where(odd, group1, group0), jnp.where(odd, group0, group1)
    half = QPG * DH
    q_mine = jnp.where(odd, queries[:, half:], queries[:, :half])
    q_other = jnp.where(odd, queries[:, :half], queries[:, half:])

    from1, from2, from3 = flip_x(other, 1), flip_x(mine, 2), flip_x(other, 3)
    units = [mine, from1, from2, from3]
    unit_a = jnp.concatenate([u[:SPAN] for u in units], axis=0)
    unit_b = jnp.concatenate([u[SPAN:] for u in units], axis=0)
    q_other, unit_a, unit_b = lax.optimization_barrier((q_other, unit_a, unit_b))

    a_below, a_above, a_far = gather_ring(unit_a, "y", core)
    b_below, b_above, b_far = gather_ring(unit_b, "z", core)
    q_partner = flip_x(q_other, 1)
    plane_a = jnp.concatenate([unit_a, a_below, a_above, a_far()], axis=0)
    plane_b = jnp.concatenate([unit_b, b_below, b_above, b_far()], axis=0)

    xs = x ^ jnp.arange(4, dtype=jnp.int32)
    turns = jnp.array([0, -1, 1, 2], jnp.int32)
    ys, zs = (y + turns) % 4, (z + turns) % 4

    def slots(kind, far, c):
        if kind == "a":
            d = device_id(xs[None, :], ys[:, None], zs[far], c)
        else:
            d = device_id(xs[None, :], ys[far], zs[:, None], c)
        return (2 * d + (0 if kind == "a" else 1)).reshape(-1)

    order = []
    for far in ((0,), (1, 2), (3,)):
        for c in (core, 1 - core):
            order += [slots(kind, f, c) for kind in ("a", "b") for f in far]
    key_spans = rows_of(span_order, jnp.concatenate(order))
    me, partner = device_id(x, y, z, core), device_id(x ^ 1, y, z, core)
    query_spans = rows_of(span_order, jnp.stack([2 * me, 2 * me + 1, 2 * partner, 2 * partner + 1]))
    ends = jnp.cumsum(doc_lengths)
    docs = jnp.concatenate([ends, doc_lengths]).astype(jnp.int32)
    lists = make_lists(key_spans, query_spans, ends, doc_lengths)

    def lists_of(stage, side):
        part = slice(0, 2) if side == 0 else slice(2, 4)
        ids, kps, cnt = lists[stage]
        return ids[part], kps[part], cnt[part], query_spans[part] * SPAN

    a_below, a_above, a_far = gather_ring(plane_a, "z", core)
    b_below, b_above, b_far = gather_ring(plane_b, "y", core)
    near = [jnp.concatenate([plane_a, plane_b], axis=0)]
    near.append(swap_core(near[0]))
    sides = (q_mine, q_partner)
    state = [attend(lists_of(0, i), docs, sides[i], near, None, True, False) for i in range(2)]
    middle = [jnp.concatenate([a_below, a_above, b_below, b_above], axis=0)]
    middle.append(swap_core(middle[0]))
    a_last, b_last = a_far(), b_far()
    state = [attend(lists_of(1, i), docs, sides[i], middle, state[i], False, False) for i in range(2)]
    final = [jnp.concatenate([a_last, b_last], axis=0)]
    final.append(swap_core(final[0]))
    o_partner, l_partner = attend(lists_of(2, 1), docs, sides[1], final, state[1], False, True)
    o_back, l_back = flip_x(o_partner, 1), flip_x(l_partner, 1)
    o_mine, l_mine = attend(lists_of(2, 0), docs, sides[0], final, state[0], False, True)

    attended = jnp.concatenate([jnp.where(odd, o_back, o_mine), jnp.where(odd, o_mine, o_back)], axis=1)
    log_sum = jnp.concatenate([jnp.where(odd, l_back, l_mine), jnp.where(odd, l_mine, l_back)], axis=1)
    return attended, log_sum.transpose(1, 0, 2).reshape(2 * QPG, 2 * SPAN)


def solution(mesh):
    rows = P(AXES, None)
    return jax.shard_map(
        on_device,
        mesh=mesh,
        in_specs=(rows, rows, rows, P(), P()),
        out_specs=(rows, P(None, AXES)),
        check_vma=False,
    )
```

```python
import functools
import itertools
import math

import jax
import jax.numpy as jnp
import numpy as np
from jax import lax
from jax.experimental import pallas as pl
from jax.experimental.pallas import tpu as pltpu
from jax.sharding import PartitionSpec as P

DH = 128
SPAN = 96
QPG = 8
MROWS = QPG * SPAN
STEP = 16
UNIT = 4
MT = 192
LOG2E = 1.0 / math.log(2.0)
SCALE2 = LOG2E / DH**0.5
M_INIT = -1e29
BIAS = -3e30
AXES = ("outer", "inner")
SETS = (64, 64, 48, 48, 32)
PACK = 128
ABSENT = 512 * PACK
F32, BF16 = jnp.float32, jnp.bfloat16


def device_id(x, y, z, c):
    return (y * 2 + z % 2) * 16 + x * 4 + (z // 2) * 2 + c


def permute(v, move):
    pairs = []
    for y, x, z, c in itertools.product(range(4), range(4), range(4), range(2)):
        pairs.append((device_id(x, y, z, c), device_id(*move(x, y, z, c))))
    return lax.ppermute(v, AXES, pairs)


def shift(v, axis, step0, step1):
    def move(x, y, z, c):
        step = step0 if c == 0 else step1
        if axis == "y":
            return x, (y + step) % 4, z, c
        return x, y, (z + step) % 4, c

    return permute(v, move)


def flip_x(v, bits):
    return permute(v, lambda x, y, z, c: (x ^ bits, y, z, c))


def swap_core(v):
    return permute(v, lambda x, y, z, c: (x, y, z, 1 - c))


def kernel(n_pieces, first, last, at, side, lists, cnt, qb, docs, q_ref, *rest):
    ends = [docs[0]]
    for j in range(1, 4):
        ends.append(ends[-1] + docs[j])
    pieces, rest = rest[:n_pieces], rest[n_pieces:]
    if not first:
        (m_in, l_in, a_in), rest = rest[:3], rest[3:]
    if last:
        (o_ref, lse_ref), rest = rest[:2], rest[2:]
    else:
        (m_out, l_out, a_out), rest = rest[:3], rest[3:]
    kv, qs, sems, *held = rest
    sp = pl.program_id(0) + side
    m_s, l_s, a_s = held if last else (r.at[sp] for r in (m_out, l_out, a_out))

    def copies():
        start, out = 0, []
        for i, piece in enumerate(pieces):
            rows = piece.shape[0]
            out.append(pltpu.make_async_copy(piece, kv.at[pl.ds(start, rows)], sems.at[i]))
            start += rows
        return out

    @pl.when(pl.program_id(0) == 0)
    def _():
        for copy in copies():
            copy.start()

    for h in range(QPG):
        qs[h * SPAN : (h + 1) * SPAN, :] = q_ref[:, h * DH : (h + 1) * DH]
    if first:
        m_s[...] = jnp.full_like(m_s, M_INIT)
        l_s[...] = jnp.zeros_like(l_s)
        a_s[...] = jnp.zeros_like(a_s)
    if last:
        m_s[...] = m_in[sp]
        l_s[...] = l_in[sp]
        a_s[...] = a_in[sp]

    @pl.when(pl.program_id(0) == 0)
    def _():
        for copy in copies():
            copy.wait()

    def step(base, count):
        nk = count * SPAN
        entries = [lists[sp, at + base + j] for j in range(count)]
        starts = [pl.multiple_of((e % PACK) * SPAN, 32) for e in entries]
        k = jnp.concatenate([kv[pl.ds(s, SPAN), 0:DH] for s in starts], axis=0)
        v = jnp.concatenate([kv[pl.ds(s, SPAN), DH : 2 * DH] for s in starts], axis=0)
        v = jnp.concatenate([v, jnp.ones_like(v)], axis=1)
        lane = lax.broadcasted_iota(jnp.int32, (8, nk), 1)
        kpos = lane
        for j in range(count):
            kpos = jnp.where(lane >= j * SPAN, lane + ((entries[j] // PACK) * SPAN - j * SPAN), kpos)
        kpos = jnp.concatenate([kpos] * (SPAN // 8), axis=0)
        qpos = lax.broadcasted_iota(jnp.int32, (SPAN, DH), 0) + qb[sp]
        start = jnp.zeros((SPAN, DH), jnp.int32)
        for j in range(4):
            start = start + jnp.where(qpos >= ends[j], docs[j], 0)
        qpos = jnp.concatenate([qpos] * (nk // DH), axis=1)
        start = jnp.concatenate([start] * (nk // DH), axis=1)
        bias = jnp.where((kpos <= qpos) & (kpos >= start), 0.0, BIAS)
        tiles = [slice(t * MT, (t + 1) * MT) for t in range(MROWS // MT)]
        scores = []
        for rows in tiles:
            s = lax.dot_general(qs[rows, :], k, (((1,), (1,)), ((), ())), preferred_element_type=F32)
            scores.append((s.reshape(MT // SPAN, SPAN, nk) + bias[None]).reshape(MT, nk))
        for rows, s in zip(tiles, scores):
            m_old = m_s[rows, :]
            m_new = jnp.maximum(m_old, jnp.max(s, axis=1, keepdims=True) * SCALE2)
            factor = jnp.exp2(m_old - m_new)
            m_s[rows, :] = m_new
            w = [jnp.exp2(s[:, j * DH : (j + 1) * DH] * SCALE2 - m_new).astype(BF16) for j in range(nk // DH)]
            both = jnp.dot(jnp.concatenate(w, axis=1), v, preferred_element_type=F32)
            a_s[rows, :] = a_s[rows, :] * factor + both[:, :DH]
            l_s[rows, :] = l_s[rows, :] * factor + both[:, DH:]

    units = (cnt[sp, STAGE_OF[at]] + (UNIT - 1)) // UNIT
    per = STEP // UNIT
    n_full = units // per

    @pl.loop(0, n_full)
    def _(number):
        step(number * STEP, STEP)

    for left in range(1, per):

        @pl.when(units - n_full * per == left)
        def _():
            step(n_full * STEP, left * UNIT)

    if last:
        for h in range(QPG):
            rows = slice(h * SPAN, (h + 1) * SPAN)
            total = l_s[rows, :]
            o_ref[:, h * DH : (h + 1) * DH] = (a_s[rows, :] / total).astype(BF16)
            lse = m_s[rows, :] * math.log(2.0) + jnp.log(total)
            lse_ref[0, h : h + 1, :] = jnp.transpose(lse)[0:1, :]


STAGE_OF = {sum(SETS[:i]): i for i in range(len(SETS))}


def attend(scalars, q, pieces, state, stage, side=0, spans=4):
    first, last = state is None, spans == 2
    total = sum(p.shape[0] for p in pieces)
    state_spec = pl.BlockSpec(memory_space=pltpu.VMEM)
    state_shape = jax.ShapeDtypeStruct((spans, MROWS, DH), F32)
    if last:
        out_specs = (
            pl.BlockSpec((SPAN, QPG * DH), lambda i, *_: (i, 0)),
            pl.BlockSpec((1, QPG, SPAN), lambda i, *_: (i, 0, 0)),
        )
        out_shape = (
            jax.ShapeDtypeStruct((spans * SPAN, QPG * DH), BF16),
            jax.ShapeDtypeStruct((spans, QPG, SPAN), F32),
        )
    else:
        out_specs, out_shape = (state_spec,) * 3, (state_shape,) * 3
    pairs = spans * MROWS * total // 3
    return pl.pallas_call(
        functools.partial(kernel, len(pieces), first, last, sum(SETS[:stage]), side),
        grid_spec=pltpu.PrefetchScalarGridSpec(
            num_scalar_prefetch=4,
            grid=(spans,),
            in_specs=[pl.BlockSpec((SPAN, QPG * DH), lambda i, *_: (i + side, 0))]
            + [pl.BlockSpec(memory_space=pl.ANY)] * len(pieces)
            + ([] if first else [state_spec] * 3),
            out_specs=out_specs,
            scratch_shapes=[
                pltpu.VMEM((total, 2 * DH), BF16),
                pltpu.VMEM((MROWS, DH), BF16),
                pltpu.SemaphoreType.DMA((len(pieces),)),
            ]
            + [pltpu.VMEM((MROWS, DH), F32)] * (3 if last else 0),
        ),
        out_shape=out_shape,
        input_output_aliases={} if first or last else {5 + len(pieces) + i: i for i in range(3)},
        compiler_params=pltpu.CompilerParams(vmem_limit_bytes=40 * 1024 * 1024),
        cost_estimate=pl.CostEstimate(flops=8 * pairs * DH, bytes_accessed=total * 512, transcendentals=pairs),
    )(*scalars, q, *pieces, *(() if first else state))


def slot_table():
    table = np.zeros((128, sum(SETS) + 4), np.int32)
    for y, x, z, c in itertools.product(range(4), range(4), range(4), range(2)):
        xs = [x ^ i for i in range(4)]
        ys, zs = ([(v + turn) % 4 for turn in (0, -1, 1, 2)] for v in (y, z))
        row = []
        for far in ((0,), (1, 2), (3,)):
            for core in (c, 1 - c):
                for f in far:
                    row += [2 * device_id(i, j, zs[f], core) for j in ys for i in xs]
                for f in far:
                    row += [2 * device_id(i, ys[f], k, core) + 1 for k in zs for i in xs]
        me, partner = device_id(x, y, z, c), device_id(x ^ 1, y, z, c)
        table[me] = row + [2 * me, 2 * me + 1, 2 * partner, 2 * partner + 1]
    return table


def make_lists(key_spans, query_spans, doc_lengths):
    n = key_spans.shape[0]
    number = np.arange(n, dtype=np.int32)
    stage = np.repeat(np.arange(len(SETS), dtype=np.int32), SETS)
    offset = np.repeat(np.array([sum(SETS[:i]) for i in range(len(SETS))], np.int32), SETS)
    a = key_spans * SPAN
    b = query_spans * SPAN
    each = np.arange(4)
    ends = jnp.sum(jnp.where(each[None, :] <= each[:, None], doc_lengths[None, :], 0), axis=1)
    first = jnp.sum(jnp.where(ends[None, :] <= b[:, None], doc_lengths[None, :], 0), axis=1)
    seen = (a[None, :] <= b[:, None] + SPAN - 1) & (a[None, :] + SPAN - 1 >= first[:, None])
    before = (stage[:, None] == stage[None, :]) & (number[None, :] < number[:, None])
    place = offset[None, :] + jnp.sum((seen[:, None, :] & before[None]).astype(jnp.int32), axis=2)
    place = jnp.where(seen, place, -1)
    packed = key_spans * PACK + number - offset - ABSENT
    hit = place[:, None, :] == number[None, :, None]
    lists = jnp.sum(jnp.where(hit, packed[None, None, :], 0), axis=2) + ABSENT
    here = stage[None, :] == jnp.arange(len(SETS), dtype=jnp.int32)[:, None]
    counts = jnp.sum((seen[:, None, :] & here[None]).astype(jnp.int32), axis=2)
    return lists, counts


def neighbours(a, b, axis_a, axis_b):
    return shift(a, axis_a, 1, 1), shift(a, axis_a, -1, -1), shift(b, axis_b, 1, 1), shift(b, axis_b, -1, -1)


def opposite(near, core, axis_a, axis_b):
    a_below, a_above, b_below, b_above = near
    a = shift(jnp.where(core == 0, a_below, a_above), axis_a, 1, -1)
    return a, shift(jnp.where(core == 0, b_below, b_above), axis_b, 1, -1)


def hold(state, arrays):
    out = lax.optimization_barrier((*state, *arrays))
    return out[:3], out[3:]


def on_device(queries, keys, values, span_order, doc_lengths):
    outer, inner = lax.axis_index("outer"), lax.axis_index("inner")
    core = inner & 1
    odd = (inner & 4) != 0

    slots = lax.dynamic_index_in_dim(jnp.asarray(slot_table()), outer * 16 + inner, 0, keepdims=False)
    slot_ids = np.arange(span_order.shape[0], dtype=np.int32)
    spans = jnp.sum(jnp.where(slots[:, None] == slot_ids[None, :], span_order[None, :], 0), axis=1)
    lists, counts = make_lists(spans[:-4], spans[-4:], doc_lengths)
    scalars = (lists, counts, spans[-4:] * SPAN, doc_lengths)

    group0 = jnp.concatenate([keys[:, :DH], values[:, :DH]], axis=1)
    group1 = jnp.concatenate([keys[:, DH:], values[:, DH:]], axis=1)
    mine, other = jnp.where(odd, group1, group0), jnp.where(odd, group0, group1)
    half = QPG * DH

    units = [mine, flip_x(other, 1), flip_x(mine, 2), flip_x(other, 3)]
    unit_a = jnp.concatenate([u[:SPAN] for u in units], axis=0)
    unit_b = jnp.concatenate([u[SPAN:] for u in units], axis=0)
    queries, unit_a, unit_b = lax.optimization_barrier((queries, unit_a, unit_b))

    q_mine = jnp.where(odd, queries[:, half:], queries[:, :half])
    q_partner = flip_x(jnp.where(odd, queries[:, :half], queries[:, half:]), 1)
    *near, q_partner = lax.optimization_barrier((*neighbours(unit_a, unit_b, "y", "z"), q_partner))
    far_a, far_b = opposite(near, core, "y", "z")
    q = jnp.concatenate([q_mine, q_partner], axis=0)
    plane_a = jnp.concatenate([unit_a, near[0], near[1], far_a], axis=0)
    plane_b = jnp.concatenate([unit_b, near[2], near[3], far_b], axis=0)
    plane_a, plane_b = lax.optimization_barrier((plane_a, plane_b))

    mine = [plane_a, plane_b]
    state = attend(scalars, q, mine + [swap_core(v) for v in mine], None, 0)
    near = neighbours(plane_a, plane_b, "z", "y")
    state, near = hold(state, near)
    far = opposite(near, core, "z", "y")
    theirs = [swap_core(v) for v in near[:3]]
    state = attend(scalars, q, near, state, 1)
    state, last = hold(state, near[3:])
    state = attend(scalars, q, theirs, state, 2)
    state, far = hold(state, far)
    theirs = [swap_core(v) for v in far]
    state = attend(scalars, q, [swap_core(last[0]), *far], state, 3)
    o_partner, l_partner = attend(scalars, q, theirs, state, 4, 2, 2)
    o_back = flip_x(o_partner, 1)
    l_back = flip_x(l_partner, 1)
    o_mine, l_mine = attend(scalars, q, theirs, state, 4, 0, 2)

    attended = jnp.concatenate([jnp.where(odd, o_back, o_mine), jnp.where(odd, o_mine, o_back)], axis=1)
    log_sum = jnp.concatenate([jnp.where(odd, l_back, l_mine), jnp.where(odd, l_mine, l_back)], axis=1)
    return attended, log_sum.transpose(1, 0, 2).reshape(2 * QPG, 2 * SPAN)


def solution(mesh):
    rows = P(AXES, None)
    return jax.shard_map(
        on_device,
        mesh=mesh,
        in_specs=(rows, rows, rows, P(), P()),
        out_specs=(rows, P(None, AXES)),
        check_vma=False,
    )
```

```python
import functools
import itertools
import math

import jax
import jax.numpy as jnp
import numpy as np
from jax import lax
from jax.experimental import pallas as pl
from jax.experimental.pallas import tpu as pltpu
from jax.sharding import PartitionSpec as P

DH = 128
SPAN = 96
QPG = 8
MROWS = QPG * SPAN
STEP = 16
UNIT = 4
MT = 192
LOG2E = 1.0 / math.log(2.0)
SCALE2 = LOG2E / DH**0.5
M_INIT = -1e29
BIAS = -3e30
AXES = ("outer", "inner")
TURNS = (0, -1, 1, 2)
SETS = (64, 64, 64, 32, 32)
OWN_SETS = (64, 64, 128)
PACK = 256
ABSENT = 512 * PACK
F32, BF16 = jnp.float32, jnp.bfloat16


def device_id(x, y, z, c):
    return (y * 2 + z % 2) * 16 + x * 4 + (z // 2) * 2 + c


def permute(v, move):
    pairs = []
    for y, x, z, c in itertools.product(range(4), range(4), range(4), range(2)):
        pairs.append((device_id(x, y, z, c), device_id(*move(x, y, z, c))))
    return lax.ppermute(v, AXES, pairs)


def shift(v, axes, step):
    def move(x, y, z, c):
        if axes[c] == "y":
            return x, (y + step) % 4, z, c
        return x, y, (z + step) % 4, c

    return permute(v, move)


def flip_x(v, bits):
    return permute(v, lambda x, y, z, c: (x ^ bits, y, z, c))


def swap_core(v):
    return permute(v, lambda x, y, z, c: (x, y, z, 1 - c))


def kernel(n_pieces, first, last, stage, at, side, lists, cnt, qb, docs, q_ref, *rest):
    ends = [docs[0]]
    for j in range(1, 4):
        ends.append(ends[-1] + docs[j])
    pieces, rest = rest[:n_pieces], rest[n_pieces:]
    if not first:
        (m_in, l_in, a_in), rest = rest[:3], rest[3:]
    if last:
        (o_ref, lse_ref), rest = rest[:2], rest[2:]
    else:
        (m_out, l_out, a_out), rest = rest[:3], rest[3:]
    kv, qs, sems, *held = rest
    sp = pl.program_id(0) + side
    m_s, l_s, a_s = held if last else (r.at[sp] for r in (m_out, l_out, a_out))

    def copies():
        start, out = 0, []
        for i, piece in enumerate(pieces):
            rows = piece.shape[0]
            out.append(pltpu.make_async_copy(piece, kv.at[pl.ds(start, rows)], sems.at[i]))
            start += rows
        return out

    @pl.when(pl.program_id(0) == 0)
    def _():
        for copy in copies():
            copy.start()

    for h in range(QPG):
        qs[h * SPAN : (h + 1) * SPAN, :] = q_ref[:, h * DH : (h + 1) * DH]
    if first:
        m_s[...] = jnp.full_like(m_s, M_INIT)
        l_s[...] = jnp.zeros_like(l_s)
        a_s[...] = jnp.zeros_like(a_s)
    if last:
        m_s[...] = m_in[sp]
        l_s[...] = l_in[sp]
        a_s[...] = a_in[sp]

    @pl.when(pl.program_id(0) == 0)
    def _():
        for copy in copies():
            copy.wait()

    def step(base, count):
        nk = count * SPAN
        entries = [lists[sp, at + base + j] for j in range(count)]
        starts = [pl.multiple_of((e % PACK) * SPAN, 32) for e in entries]
        k = jnp.concatenate([kv[pl.ds(s, SPAN), 0:DH] for s in starts], axis=0)
        v = jnp.concatenate([kv[pl.ds(s, SPAN), DH : 2 * DH] for s in starts], axis=0)
        v = jnp.concatenate([v, jnp.ones_like(v)], axis=1)
        lane = lax.broadcasted_iota(jnp.int32, (8, nk), 1)
        kpos = lane
        for j in range(count):
            kpos = jnp.where(lane >= j * SPAN, lane + ((entries[j] // PACK) * SPAN - j * SPAN), kpos)
        kpos = jnp.concatenate([kpos] * (SPAN // 8), axis=0)
        qpos = lax.broadcasted_iota(jnp.int32, (SPAN, DH), 0) + qb[sp]
        start = jnp.zeros((SPAN, DH), jnp.int32)
        for j in range(4):
            start = start + jnp.where(qpos >= ends[j], docs[j], 0)
        qpos = jnp.concatenate([qpos] * (nk // DH), axis=1)
        start = jnp.concatenate([start] * (nk // DH), axis=1)
        bias = jnp.where((kpos <= qpos) & (kpos >= start), 0.0, BIAS)
        tiles = [slice(t * MT, (t + 1) * MT) for t in range(MROWS // MT)]
        scores = []
        for rows in tiles:
            s = lax.dot_general(qs[rows, :], k, (((1,), (1,)), ((), ())), preferred_element_type=F32)
            scores.append((s.reshape(MT // SPAN, SPAN, nk) + bias[None]).reshape(MT, nk))
        for rows, s in zip(tiles, scores):
            m_old = m_s[rows, :]
            m_new = jnp.maximum(m_old, jnp.max(s, axis=1, keepdims=True) * SCALE2)
            factor = jnp.exp2(m_old - m_new)
            m_s[rows, :] = m_new
            w = [jnp.exp2(s[:, j * DH : (j + 1) * DH] * SCALE2 - m_new).astype(BF16) for j in range(nk // DH)]
            both = jnp.dot(jnp.concatenate(w, axis=1), v, preferred_element_type=F32)
            a_s[rows, :] = a_s[rows, :] * factor + both[:, :DH]
            l_s[rows, :] = l_s[rows, :] * factor + both[:, DH:]

    units = (cnt[sp, stage] + (UNIT - 1)) // UNIT
    per = STEP // UNIT
    n_full = units // per

    @pl.loop(0, n_full)
    def _(number):
        step(number * STEP, STEP)

    for left in range(1, per):

        @pl.when(units - n_full * per == left)
        def _():
            step(n_full * STEP, left * UNIT)

    if last:
        for h in range(QPG):
            rows = slice(h * SPAN, (h + 1) * SPAN)
            total = l_s[rows, :]
            o_ref[:, h * DH : (h + 1) * DH] = (a_s[rows, :] / total).astype(BF16)
            lse = m_s[rows, :] * math.log(2.0) + jnp.log(total)
            lse_ref[0, h : h + 1, :] = jnp.transpose(lse)[0:1, :]


def attend(scalars, q, pieces, state, stage, side, spans, last=False):
    first = state is None
    total = sum(p.shape[0] for p in pieces)
    state_spec = pl.BlockSpec(memory_space=pltpu.VMEM)
    state_shape = jax.ShapeDtypeStruct((4, MROWS, DH), F32)
    if last:
        out_specs = (
            pl.BlockSpec((SPAN, QPG * DH), lambda i, *_: (i, 0)),
            pl.BlockSpec((1, QPG, SPAN), lambda i, *_: (i, 0, 0)),
        )
        out_shape = (
            jax.ShapeDtypeStruct((spans * SPAN, QPG * DH), BF16),
            jax.ShapeDtypeStruct((spans, QPG, SPAN), F32),
        )
    else:
        out_specs, out_shape = (state_spec,) * 3, (state_shape,) * 3
    pairs = spans * MROWS * total // 3
    return pl.pallas_call(
        functools.partial(kernel, len(pieces), first, last, stage, sum(SETS[:stage]), side),
        grid_spec=pltpu.PrefetchScalarGridSpec(
            num_scalar_prefetch=4,
            grid=(spans,),
            in_specs=[pl.BlockSpec((SPAN, QPG * DH), lambda i, *_: (i + side, 0))]
            + [pl.BlockSpec(memory_space=pl.ANY)] * len(pieces)
            + ([] if first else [state_spec] * 3),
            out_specs=out_specs,
            scratch_shapes=[
                pltpu.VMEM((total, 2 * DH), BF16),
                pltpu.VMEM((MROWS, DH), BF16),
                pltpu.SemaphoreType.DMA((len(pieces),)),
            ]
            + [pltpu.VMEM((MROWS, DH), F32)] * (3 if last else 0),
        ),
        out_shape=out_shape,
        input_output_aliases={} if first or last else {5 + len(pieces) + i: i for i in range(3)},
        compiler_params=pltpu.CompilerParams(vmem_limit_bytes=40 * 1024 * 1024),
        cost_estimate=pl.CostEstimate(flops=8 * pairs * DH, bytes_accessed=total * 512, transcendentals=pairs),
    )(*scalars, q, *pieces, *(() if first else state))


def slot_table():
    table = np.zeros((128, sum(SETS) + 4), np.int32)
    for y, x, z, c in itertools.product(range(4), range(4), range(4), range(2)):

        def plane(holder, far):
            out = []
            for near, i, core in itertools.product(TURNS, range(4), (holder, 1 - holder)):
                up, along = (near, far) if holder == 0 else (far, near)
                out.append(2 * device_id(x ^ i, (y + up) % 4, (z + along) % 4, core) + holder)
            return out

        row = []
        for turns in ((0,), (-1, 1), (2,)):
            for holder in (c, 1 - c):
                for far in turns:
                    row += plane(holder, far)
        me, partner = device_id(x, y, z, c), device_id(x ^ 1, y, z, c)
        table[me] = row + [2 * me, 2 * me + 1, 2 * partner, 2 * partner + 1]
    return table


def make_lists(key_spans, query_spans, doc_lengths):
    n = key_spans.shape[0]
    number = np.arange(n, dtype=np.int32)
    sets = (OWN_SETS, OWN_SETS, SETS, SETS)
    stage = np.stack([np.repeat(np.arange(len(v), dtype=np.int32), v) for v in sets])
    offset = np.stack([np.repeat(np.cumsum((0,) + v[:-1], dtype=np.int32), v) for v in sets])
    a = key_spans * SPAN
    b = query_spans * SPAN
    each = np.arange(4)
    ends = jnp.sum(jnp.where(each[None, :] <= each[:, None], doc_lengths[None, :], 0), axis=1)
    first = jnp.sum(jnp.where(ends[None, :] <= b[:, None], doc_lengths[None, :], 0), axis=1)
    seen = (a[None, :] <= b[:, None] + SPAN - 1) & (a[None, :] + SPAN - 1 >= first[:, None])
    before = (stage[:, :, None] == stage[:, None, :]) & (number[None, None, :] < number[None, :, None])
    place = offset + jnp.sum((seen[:, None, :] & before).astype(jnp.int32), axis=2)
    place = jnp.where(seen, place, -1)
    packed = (key_spans * PACK)[None, :] + (number[None, :] - offset - ABSENT)
    hit = place[:, None, :] == number[None, :, None]
    lists = jnp.sum(jnp.where(hit, packed[:, None, :], 0), axis=2) + ABSENT
    here = stage[:, None, :] == np.arange(len(SETS), dtype=np.int32)[None, :, None]
    counts = jnp.sum((seen[:, None, :] & here).astype(jnp.int32), axis=2)
    return lists, counts


def neighbours(v, axes):
    return [shift(v, axes, 1), shift(v, axes, -1)]


def opposite(near, axes):
    half = near[0].shape[0] // 2
    return [shift(near[0][:half], axes, 1), shift(near[1][half:], axes, -1)]


def hold(state, arrays):
    out = lax.optimization_barrier((*state, *arrays))
    return out[:3], out[3:]


def on_device(queries, keys, values, span_order, doc_lengths):
    outer, inner = lax.axis_index("outer"), lax.axis_index("inner")
    core = inner & 1
    odd = (inner & 4) != 0

    slots = lax.dynamic_index_in_dim(jnp.asarray(slot_table()), outer * 16 + inner, 0, keepdims=False)
    slot_ids = np.arange(span_order.shape[0], dtype=np.int32)
    spans = jnp.sum(jnp.where(slots[:, None] == slot_ids[None, :], span_order[None, :], 0), axis=1)
    lists, counts = make_lists(spans[:-4], spans[-4:], doc_lengths)
    scalars = (lists, counts, spans[-4:] * SPAN, doc_lengths)

    both = jnp.concatenate([keys[:, :DH], values[:, :DH], keys[:, DH:], values[:, DH:]], axis=1)
    kept, given = (jnp.where(core == i, both[:SPAN], both[SPAN:]) for i in (0, 1))
    both = jnp.concatenate([kept, swap_core(given)], axis=0)

    mine = jnp.where(odd, both[:, 2 * DH :], both[:, : 2 * DH])
    other = jnp.where(odd, both[:, : 2 * DH], both[:, 2 * DH :])
    unit = jnp.concatenate([mine, flip_x(other, 1), flip_x(mine, 2), flip_x(other, 3)], axis=0)
    queries, unit = lax.optimization_barrier((queries, unit))

    half = QPG * DH
    q_mine = jnp.where(odd, queries[:, half:], queries[:, :half])
    q_other = jnp.where(odd, queries[:, :half], queries[:, half:])
    q_first = flip_x(q_other[:SPAN], 1)
    *near, q_first = lax.optimization_barrier((*neighbours(unit, "yz"), q_first))
    q_second = flip_x(q_other[SPAN:], 1)
    plane = jnp.concatenate([unit, *near, *opposite(near, "yz")], axis=0)
    plane, q_second = lax.optimization_barrier((plane, q_second))
    q = jnp.concatenate([q_mine, q_first, q_second], axis=0)

    state = attend(scalars, q, [plane, swap_core(plane)], None, 0, 0, 4)
    state, near = hold(state, neighbours(plane, "zy"))
    far = opposite(near, "zy")
    theirs = [swap_core(v) for v in near]
    state = attend(scalars, q, near, state, 1, 0, 4)
    state = attend(scalars, q, theirs, state, 2, 2, 2)
    state, far = hold(state, far)
    far_theirs = [swap_core(v) for v in far]
    state = attend(scalars, q, far, state, 3, 2, 2)
    o_partner, l_partner = attend(scalars, q, far_theirs, state, 4, 2, 2, True)
    o_back = flip_x(o_partner, 1)
    l_back = flip_x(l_partner, 1)
    o_mine, l_mine = attend(scalars, q, [*theirs, *far, *far_theirs], state, 2, 0, 2, True)

    attended = jnp.concatenate([jnp.where(odd, o_back, o_mine), jnp.where(odd, o_mine, o_back)], axis=1)
    log_sum = jnp.concatenate([jnp.where(odd, l_back, l_mine), jnp.where(odd, l_mine, l_back)], axis=1)
    return attended, log_sum.transpose(1, 0, 2).reshape(2 * QPG, 2 * SPAN)


def solution(mesh):
    rows = P(AXES, None)
    return jax.shard_map(
        on_device,
        mesh=mesh,
        in_specs=(rows, rows, rows, P(), P()),
        out_specs=(rows, P(None, AXES)),
        check_vma=False,
    )
```

```python
import functools
import itertools
import math

import jax
import jax.numpy as jnp
import numpy as np
from jax import lax
from jax.experimental import pallas as pl
from jax.experimental.pallas import tpu as pltpu
from jax.sharding import PartitionSpec as P

DH = 128
SPAN = 96
QPG = 8
MROWS = QPG * SPAN
STEP = 12
UNIT = 4
MT = 192
LOG2E = 1.0 / math.log(2.0)
SCALE2 = LOG2E / DH**0.5
M_INIT = -1e29
BIAS = -3e30
AXES = ("outer", "inner")
TURNS = (0, -1, 1, 2)
SETS = (64, 64, 64, 32, 32)
OWN_SETS = (64, 64, 128)
PACK = 256
ABSENT = 512 * PACK
F32, BF16 = jnp.float32, jnp.bfloat16


def device_id(x, y, z, c):
    return (y * 2 + z % 2) * 16 + x * 4 + (z // 2) * 2 + c


def permute(v, move):
    pairs = []
    for y, x, z, c in itertools.product(range(4), range(4), range(4), range(2)):
        pairs.append((device_id(x, y, z, c), device_id(*move(x, y, z, c))))
    return lax.ppermute(v, AXES, pairs)


def shift(v, axes, step):
    def move(x, y, z, c):
        if axes[c] == "y":
            return x, (y + step) % 4, z, c
        return x, y, (z + step) % 4, c

    return permute(v, move)


def flip_x(v, bits):
    return permute(v, lambda x, y, z, c: (x ^ bits, y, z, c))


def swap_core(v):
    return permute(v, lambda x, y, z, c: (x, y, z, 1 - c))


def kernel(n_pieces, first, last, stage, at, side, lists, cnt, qb, docs, q_ref, *rest):
    ends = [docs[0]]
    for j in range(1, 4):
        ends.append(ends[-1] + docs[j])
    pieces, rest = rest[:n_pieces], rest[n_pieces:]
    if not first:
        (m_in, l_in, a_in), rest = rest[:3], rest[3:]
    if last:
        (o_ref, lse_ref), rest = rest[:2], rest[2:]
    else:
        (m_out, l_out, a_out), rest = rest[:3], rest[3:]
    kv, qs, sems, *held = rest
    sp = pl.program_id(0) + side
    m_s, l_s, a_s = held if last else (r.at[sp] for r in (m_out, l_out, a_out))

    def copies():
        start, out = 0, []
        for i, piece in enumerate(pieces):
            rows = piece.shape[0]
            out.append(pltpu.make_async_copy(piece, kv.at[pl.ds(start, rows)], sems.at[i]))
            start += rows
        return out

    @pl.when(pl.program_id(0) == 0)
    def _():
        for copy in copies():
            copy.start()

    for h in range(QPG):
        qs[h * SPAN : (h + 1) * SPAN, :] = q_ref[:, h * DH : (h + 1) * DH]
    if first:
        m_s[...] = jnp.full_like(m_s, M_INIT)
        l_s[...] = jnp.zeros_like(l_s)
        a_s[...] = jnp.zeros_like(a_s)
    if last:
        m_s[...] = m_in[sp]
        l_s[...] = l_in[sp]
        a_s[...] = a_in[sp]

    @pl.when(pl.program_id(0) == 0)
    def _():
        for copy in copies():
            copy.wait()

    def step(base, count):
        nk = count * SPAN
        entries = [lists[sp, at + base + j] for j in range(count)]
        starts = [pl.multiple_of((e % PACK) * SPAN, 32) for e in entries]
        k = jnp.concatenate([kv[pl.ds(s, SPAN), 0:DH] for s in starts], axis=0)
        v = jnp.concatenate([kv[pl.ds(s, SPAN), DH : 2 * DH] for s in starts], axis=0)
        v = jnp.concatenate([v, jnp.ones_like(v)], axis=1)
        lane = lax.broadcasted_iota(jnp.int32, (8, nk), 1)
        kpos = lane
        for j in range(count):
            kpos = jnp.where(lane >= j * SPAN, lane + ((entries[j] // PACK) * SPAN - j * SPAN), kpos)
        kpos = jnp.concatenate([kpos] * (SPAN // 8), axis=0)
        qpos = lax.broadcasted_iota(jnp.int32, (SPAN, DH), 0) + qb[sp]
        start = jnp.zeros((SPAN, DH), jnp.int32)
        for j in range(4):
            start = start + jnp.where(qpos >= ends[j], docs[j], 0)
        qpos = jnp.concatenate([qpos] * (nk // DH), axis=1)
        start = jnp.concatenate([start] * (nk // DH), axis=1)
        bias = jnp.where((kpos <= qpos) & (kpos >= start), 0.0, BIAS)
        tiles = [slice(t * MT, (t + 1) * MT) for t in range(MROWS // MT)]
        scores = []
        for rows in tiles:
            s = lax.dot_general(qs[rows, :], k, (((1,), (1,)), ((), ())), preferred_element_type=F32)
            scores.append((s.reshape(MT // SPAN, SPAN, nk) + bias[None]).reshape(MT, nk))
        for rows, s in zip(tiles, scores):
            m_old = m_s[rows, :]
            m_new = jnp.maximum(m_old, jnp.max(s, axis=1, keepdims=True) * SCALE2)
            factor = jnp.exp2(m_old - m_new)
            m_s[rows, :] = m_new
            w = [jnp.exp2(s[:, j * DH : (j + 1) * DH] * SCALE2 - m_new).astype(BF16) for j in range(nk // DH)]
            both = jnp.dot(jnp.concatenate(w, axis=1), v, preferred_element_type=F32)
            a_s[rows, :] = a_s[rows, :] * factor + both[:, :DH]
            l_s[rows, :] = l_s[rows, :] * factor + both[:, DH:]

    units = (cnt[sp, stage] + (UNIT - 1)) // UNIT
    per = STEP // UNIT
    n_full = units // per

    @pl.loop(0, n_full)
    def _(number):
        step(number * STEP, STEP)

    for left in range(1, per):

        @pl.when(units - n_full * per == left)
        def _():
            step(n_full * STEP, left * UNIT)

    if last:
        for h in range(QPG):
            rows = slice(h * SPAN, (h + 1) * SPAN)
            total = l_s[rows, :]
            o_ref[:, h * DH : (h + 1) * DH] = (a_s[rows, :] / total).astype(BF16)
            lse = m_s[rows, :] * math.log(2.0) + jnp.log(total)
            lse_ref[0, h : h + 1, :] = jnp.transpose(lse)[0:1, :]


def attend(scalars, q, pieces, state, stage, side, spans, last=False):
    first = state is None
    total = sum(p.shape[0] for p in pieces)
    state_spec = pl.BlockSpec(memory_space=pltpu.VMEM)
    state_shape = jax.ShapeDtypeStruct((4, MROWS, DH), F32)
    if last:
        out_specs = (
            pl.BlockSpec((SPAN, QPG * DH), lambda i, *_: (i, 0)),
            pl.BlockSpec((1, QPG, SPAN), lambda i, *_: (i, 0, 0)),
        )
        out_shape = (
            jax.ShapeDtypeStruct((spans * SPAN, QPG * DH), BF16),
            jax.ShapeDtypeStruct((spans, QPG, SPAN), F32),
        )
    else:
        out_specs, out_shape = (state_spec,) * 3, (state_shape,) * 3
    pairs = spans * MROWS * total // 3
    return pl.pallas_call(
        functools.partial(kernel, len(pieces), first, last, stage, sum(SETS[:stage]), side),
        grid_spec=pltpu.PrefetchScalarGridSpec(
            num_scalar_prefetch=4,
            grid=(spans,),
            in_specs=[pl.BlockSpec((SPAN, QPG * DH), lambda i, *_: (i + side, 0))]
            + [pl.BlockSpec(memory_space=pl.ANY)] * len(pieces)
            + ([] if first else [state_spec] * 3),
            out_specs=out_specs,
            scratch_shapes=[
                pltpu.VMEM((total, 2 * DH), BF16),
                pltpu.VMEM((MROWS, DH), BF16),
                pltpu.SemaphoreType.DMA((len(pieces),)),
            ]
            + [pltpu.VMEM((MROWS, DH), F32)] * (3 if last else 0),
        ),
        out_shape=out_shape,
        input_output_aliases={} if first or last else {5 + len(pieces) + i: i for i in range(3)},
        compiler_params=pltpu.CompilerParams(vmem_limit_bytes=40 * 1024 * 1024),
        cost_estimate=pl.CostEstimate(flops=8 * pairs * DH, bytes_accessed=total * 512, transcendentals=pairs),
    )(*scalars, q, *pieces, *(() if first else state))


def slot_table():
    table = np.zeros((128, sum(SETS) + 4), np.int32)
    for y, x, z, c in itertools.product(range(4), range(4), range(4), range(2)):

        def plane(holder, far):
            out = []
            for near, i, core in itertools.product(TURNS, range(4), (holder, 1 - holder)):
                up, along = (near, far) if holder == 0 else (far, near)
                out.append(2 * device_id(x ^ i, (y + up) % 4, (z + along) % 4, core) + holder)
            return out

        row = []
        for turns in ((0,), (-1, 1), (2,)):
            for holder in (c, 1 - c):
                for far in turns:
                    row += plane(holder, far)
        me, partner = device_id(x, y, z, c), device_id(x ^ 1, y, z, c)
        table[me] = row + [2 * me, 2 * me + 1, 2 * partner, 2 * partner + 1]
    return table


def make_lists(key_spans, query_spans, doc_lengths):
    n = key_spans.shape[0]
    number = np.arange(n, dtype=np.int32)
    sets = (OWN_SETS, OWN_SETS, SETS, SETS)
    stage = np.stack([np.repeat(np.arange(len(v), dtype=np.int32), v) for v in sets])
    offset = np.stack([np.repeat(np.cumsum((0,) + v[:-1], dtype=np.int32), v) for v in sets])
    a = key_spans * SPAN
    b = query_spans * SPAN
    each = np.arange(4)
    ends = jnp.sum(jnp.where(each[None, :] <= each[:, None], doc_lengths[None, :], 0), axis=1)
    first = jnp.sum(jnp.where(ends[None, :] <= b[:, None], doc_lengths[None, :], 0), axis=1)
    seen = (a[None, :] <= b[:, None] + SPAN - 1) & (a[None, :] + SPAN - 1 >= first[:, None])
    before = (stage[:, :, None] == stage[:, None, :]) & (number[None, None, :] < number[None, :, None])
    place = offset + jnp.sum((seen[:, None, :] & before).astype(jnp.int32), axis=2)
    place = jnp.where(seen, place, -1)
    packed = (key_spans * PACK)[None, :] + (number[None, :] - offset - ABSENT)
    hit = place[:, None, :] == number[None, :, None]
    lists = jnp.sum(jnp.where(hit, packed[:, None, :], 0), axis=2) + ABSENT
    here = stage[:, None, :] == np.arange(len(SETS), dtype=np.int32)[None, :, None]
    counts = jnp.sum((seen[:, None, :] & here).astype(jnp.int32), axis=2)
    return lists, counts


def neighbours(v, axes):
    return [shift(v, axes, 1), shift(v, axes, -1)]


def opposite(near, axes):
    half = near[0].shape[0] // 2
    return [shift(near[0][:half], axes, 1), shift(near[1][half:], axes, -1)]


def hold(state, arrays):
    out = lax.optimization_barrier((*state, *arrays))
    return out[:3], out[3:]


def on_device(queries, keys, values, span_order, doc_lengths):
    outer, inner = lax.axis_index("outer"), lax.axis_index("inner")
    core = inner & 1
    odd = (inner & 4) != 0

    slots = lax.dynamic_index_in_dim(jnp.asarray(slot_table()), outer * 16 + inner, 0, keepdims=False)
    slot_ids = np.arange(span_order.shape[0], dtype=np.int32)
    spans = jnp.sum(jnp.where(slots[:, None] == slot_ids[None, :], span_order[None, :], 0), axis=1)
    lists, counts = make_lists(spans[:-4], spans[-4:], doc_lengths)
    scalars = (lists, counts, spans[-4:] * SPAN, doc_lengths)

    both = jnp.concatenate([keys[:, :DH], values[:, :DH], keys[:, DH:], values[:, DH:]], axis=1)
    kept, given = (jnp.where(core == i, both[:SPAN], both[SPAN:]) for i in (0, 1))
    both = jnp.concatenate([kept, swap_core(given)], axis=0)

    mine = jnp.where(odd, both[:, 2 * DH :], both[:, : 2 * DH])
    other = jnp.where(odd, both[:, : 2 * DH], both[:, 2 * DH :])
    unit = jnp.concatenate([mine, flip_x(other, 1), flip_x(mine, 2), flip_x(other, 3)], axis=0)
    queries, unit = lax.optimization_barrier((queries, unit))

    half = QPG * DH
    q_mine = jnp.where(odd, queries[:, half:], queries[:, :half])
    q_other = jnp.where(odd, queries[:, :half], queries[:, half:])
    q_first = flip_x(q_other[:SPAN], 1)
    *near, q_first = lax.optimization_barrier((*neighbours(unit, "yz"), q_first))
    q_second = flip_x(q_other[SPAN:], 1)
    plane = jnp.concatenate([unit, *near, *opposite(near, "yz")], axis=0)
    plane, q_second = lax.optimization_barrier((plane, q_second))
    q = jnp.concatenate([q_mine, q_first, q_second], axis=0)

    state = attend(scalars, q, [plane, swap_core(plane)], None, 0, 0, 4)
    state, near = hold(state, neighbours(plane, "zy"))
    far = opposite(near, "zy")
    theirs = [swap_core(v) for v in near]
    state = attend(scalars, q, near, state, 1, 0, 4)
    state = attend(scalars, q, theirs, state, 2, 2, 2)
    state, far = hold(state, far)
    far_theirs = [swap_core(v) for v in far]
    state = attend(scalars, q, far, state, 3, 2, 2)
    o_partner, l_partner = attend(scalars, q, far_theirs, state, 4, 2, 2, True)
    o_back = flip_x(o_partner, 1)
    l_back = flip_x(l_partner, 1)
    o_mine, l_mine = attend(scalars, q, [*theirs, *far, *far_theirs], state, 2, 0, 2, True)

    attended = jnp.concatenate([jnp.where(odd, o_back, o_mine), jnp.where(odd, o_mine, o_back)], axis=1)
    log_sum = jnp.concatenate([jnp.where(odd, l_back, l_mine), jnp.where(odd, l_mine, l_back)], axis=1)
    return attended, log_sum.transpose(1, 0, 2).reshape(2 * QPG, 2 * SPAN)


def solution(mesh):
    rows = P(AXES, None)
    return jax.shard_map(
        on_device,
        mesh=mesh,
        in_specs=(rows, rows, rows, P(), P()),
        out_specs=(rows, P(None, AXES)),
        check_vma=False,
    )
```
